256 devices in a mesh: req: 8 (over y, core), exp: 32 (over z, x).
Axes of the slice: x: 4, y: 4, z: 8, core: 2. Of those that a mesh axis runs over, the one named last changes fastest.
Arguments:
- latent_cache: bfloat16 [2048, 36864], P(('req', 'exp')), may hold values from -6 to 6
- old_slot: int32 [2048], P(('req', 'exp')), may hold values from 0 to 2047, as said below
- lengths: int32 [2048], P(('req', 'exp')), may hold values from 2 to 63
- new_latent: bfloat16 [2048, 576], P(('req', 'exp')), may hold values from -6 to 6
- queries: bfloat16 [2048, 36864], P(('req', 'exp')), may hold values from -110 to 110
- hidden: bfloat16 [2048, 7168], P(('req', 'exp')), may hold values from -6 to 6
- expert_ids: int32 [2048, 8], P(('req', 'exp')), may hold values from 0 to 31, all different within a row; in each aligned block of 8 rows (0 to 7, 8 to 15, ...) at most 3 rows name the same one
- expert_gates: float32 [2048, 8], P(('req', 'exp')), may hold values from 0.05 to 0.6
- gate_weight: bfloat16 [32, 7168, 1024], P('exp', 'req'), may hold values from -0.0625 to 0.0625
- up_weight: bfloat16 [32, 7168, 1024], P('exp', 'req'), may hold values from -0.0625 to 0.0625
- down_weight: bfloat16 [32, 1024, 7168], P('exp', None, 'req'), may hold values from -0.1875 to 0.1875
Outputs:
- cache_out: bfloat16 [2048, 36864], P(('req', 'exp'))
- attention: bfloat16 [2048, 32768], P(('req', 'exp'))
- moe_out: bfloat16 [2048, 7168], P(('req', 'exp'))
The draws below stay inside these ranges and needn't reach their ends.
Inputs may be any that keep to these rules, and one draw needn't show every extreme that they name: A permutation: new row j takes the request of old row old_slot[j], which lies on the same index of exp; every device hands exactly 1 of its rows to each index of req. `expert_ids`: in the rows of one device no expert is named more than 3 times; every expert is named by some row.
All inputs are finite; a program needn't handle non-finite values.
Results may differ from the reference program's by a relative error of at most 0.029.
Values may be sent and summed in bfloat16 or wider, within the bound.
No kernel may reach another device: no remote copies, remote signals or barrier semaphores. Data moves between devices by JAX's collectives and lax.ppermute only.
A program may use at most 64 MiB of HBM per device.

```python
import math
import jax
import jax.numpy as jnp
import numpy as np
from jax import lax

D = 7168
LAT = 512
ROPE = 64
TOP = 8
KVW = 576
HEADS = 64
FF = 1024
RPP = 1
LEN = 64
EXPERTS = 32
REQ_DEV = 8
ROWS = 2048
CAP = 3
N_REQ = 8
N_EXP = 32


score_scale = 0.07216878364870323


def source_rows(key):
    key = jax.random.fold_in(key, 11)
    first_key, second_key = jax.random.split(key)
    offsets = jnp.arange(REQ_DEV, dtype=jnp.int32)
    sent_scores = jax.random.randint(first_key, (N_REQ, N_EXP, REQ_DEV), 0, 1 << 20) * REQ_DEV + offsets
    sent_order = jnp.argsort(sent_scores, axis=-1).astype(jnp.int32)
    taken_scores = jax.random.randint(second_key, (N_REQ, N_EXP, REQ_DEV), 0, 1 << 20) * REQ_DEV + offsets
    taken_order = jnp.argsort(taken_scores, axis=-1).astype(jnp.int32)
    req_index = jnp.arange(N_REQ, dtype=jnp.int32)[:, None, None]
    exp_index = jnp.arange(N_EXP, dtype=jnp.int32)[None, :, None]
    sender = taken_order // RPP
    within = taken_order % RPP
    old_pos = sent_order[sender, exp_index, req_index * RPP + within]
    return ((sender * N_EXP + exp_index) * REQ_DEV + old_pos).reshape(-1).astype(jnp.int32)


def strengths(key):
    key = jax.random.fold_in(key, 31)
    return jax.random.uniform(key, (ROWS,), jnp.float32, 30.0, 60.0)


def float_law(key, shape, mixing):
    normal_part = jnp.clip(jax.random.normal(key, shape, jnp.float32), -6.0, 6.0)
    even_part = jax.random.uniform(jax.random.fold_in(key, 5), shape, jnp.float32, -1.7, 1.7)
    return (1.0 - mixing) * normal_part + mixing * even_part


def rope_zero(key, mixing):
    key = jax.random.fold_in(key, 41)
    return float_law(key, (ROWS, ROPE), mixing)


def cache_values(key, mixing, tying):
    body_key = jax.random.fold_in(key, 43)
    values = float_law(body_key, (ROWS, LEN, KVW), mixing)
    first_rope = rope_zero(key, mixing)
    shrink = 1.0 - 2.0 / (strengths(key) * score_scale * ROPE)
    second_rope = tying * first_rope * shrink[:, None] + (1.0 - tying) * values[:, 1, LAT:]
    values = values.at[:, 0, LAT:].set(first_rope)
    values = values.at[:, 1, LAT:].set(second_rope)
    return values.reshape(ROWS, LEN * KVW)


def draw_old_slot(key, part):
    return source_rows(key)


def draw_latent_cache(key, part):
    return cache_values(key, 0.0, 0.0).astype(jnp.bfloat16)


def draw_queries(key, part):
    own_key = jax.random.fold_in(key, 7)
    return float_law(own_key, (ROWS, HEADS * KVW), 0.0).astype(jnp.bfloat16)


def plant(entries, key, smallest, high):
    shape = entries.shape
    index_at = [jax.random.randint(jax.random.fold_in(key, axis), (), 0, shape[axis]) for axis in range(len(shape))]
    entries = entries.at[tuple(index_at)].set(smallest)
    longest = shape.index(max(shape))
    index_at[longest] = (index_at[longest] + 1) % shape[longest]
    return entries.at[tuple(index_at)].set(high)


def levels(key, shape, pieces, least, top_value):
    factor_of, own = 1.0, jax.random.fold_in(key, 6)
    for position, blocks in pieces:
        draws = jnp.exp(jax.random.uniform(jax.random.fold_in(own, position), (blocks,), jnp.float32, least / len(pieces), top_value / len(pieces)))
        factor_of = factor_of * jnp.repeat(draws, shape[position] // blocks).reshape([-1 if axis == position else 1 for axis in range(len(shape))])
    return factor_of


def routed_block(rng, own, number, rows, number_of, top, most, slope):
    sequence = jax.random.permutation(rng, number_of)
    heavy_load, usual = shares(number_of, rows * top, most, slope, True), shares(number_of, rows * top, most, slope, False)
    places = jnp.arange(number_of)

    def named(sizes, rotation):
        used = int((sizes > 0).sum())
        fixed = max(1, used // 4)
        moved = fixed + (places - fixed + rotation * (used - fixed)) % max(1, number_of - fixed)
        return jnp.zeros((number_of,), jnp.int32).at[sequence[jnp.where(places < fixed, places, moved)]].set(jnp.asarray(sizes, jnp.int32))

    sizes = jnp.where(number % 4 == 0, named(heavy_load, number // 4), named(usual, number - number // 4 - 1))
    mixed = jax.random.permutation(jax.random.fold_in(own, 3), number_of)
    source_of, sink = mixed[0:number_of // 2 * 2:2], mixed[1:number_of // 2 * 2:2]
    slack = jnp.minimum(sizes[source_of] - 1, most - sizes[sink]) // 2
    slack = jnp.where((source_of == sequence[0]) | (sink == sequence[0]) | (sizes[sink] == 0), 0, jnp.maximum(slack, 0))
    moved = jax.random.randint(jax.random.fold_in(own, 4), (number_of // 2,), 0, 1 << 20) % (slack + 1)
    sizes = sizes.at[source_of].add(-moved).at[sink].add(moved)
    members = jnp.searchsorted(jnp.cumsum(sizes), jnp.arange(rows * top), side="right").astype(jnp.int32)
    grid = members.reshape(top, rows).T
    grid = grid[jax.random.permutation(jax.random.fold_in(own, 1), rows)]
    rotation = jax.random.randint(jax.random.fold_in(own, 2), (rows, 1), 0, top)
    return jnp.take_along_axis(grid, (jnp.arange(top)[None, :] + rotation) % top, axis=1)


def shares(number_of, total, reach, skew, full):
    loads = [(1 << 20) // math.isqrt(grade ** skew) + 1 for grade in range(1, number_of + 1)]
    largest = reach if full else min(reach, max(-(-total // number_of), total * loads[0] // sum(loads)))
    least = 1 if total - largest >= number_of - 1 else 0
    counts, spare = [largest] + [least] * (number_of - 1), total - largest - least * (number_of - 1)
    while spare > 0:
        free = [i for i in range(1, number_of) if counts[i] < largest] or [i for i in range(1, number_of) if counts[i] < reach]
        pool, budget = sum([loads[i] for i in free]), spare
        for i in free:
            addition = min(reach - counts[i], max(1, budget * loads[i] // pool), spare)
            counts[i] = counts[i] + addition
            spare = spare - addition
    return np.array(counts)


def gaussian(key, dims, spread, bound, pieces=(), kind=jnp.bfloat16):
    drawn = spread * jax.random.normal(key, dims, jnp.float32)
    if pieces:
        drawn = drawn * levels(key, dims, pieces, -0.22, 0.18)
    return jnp.clip(drawn, -bound, bound).astype(kind)


def setup_inputs(seed: int = 0) -> dict:
    seeds = jax.random.split(jax.random.key(seed), 12)
    latent_cache = draw_latent_cache(jax.random.fold_in(seeds[11], 71), 0)
    old_slot = draw_old_slot(jax.random.fold_in(seeds[11], 71), 0)
    lengths = plant(jax.random.randint(seeds[2], (ROWS,), 2, LEN), jax.random.fold_in(seeds[2], 1), 2, LEN - 1).astype(jnp.int32)
    new_latent = gaussian(seeds[3], (ROWS, KVW), 1.0, 6.0, ((0, 256),))
    queries = draw_queries(jax.random.fold_in(seeds[11], 71), 0)
    hidden = gaussian(seeds[5], (ROWS, D), 1.0, 6.0, ((0, 256),))
    expert_ids_keys = jax.random.split(jax.random.fold_in(seeds[6], 1), ROWS // REQ_DEV)
    expert_ids_turns = jax.random.permutation(jax.random.fold_in(seeds[6], 3), ROWS // REQ_DEV)
    expert_ids = jax.vmap(lambda own, number: routed_block(jax.random.fold_in(seeds[6], 2), own, number, REQ_DEV, EXPERTS, TOP, CAP, 2))(expert_ids_keys, expert_ids_turns).reshape((ROWS, TOP))
    expert_gates = jnp.clip(jnp.exp(math.log(0.6) - 2.4849067 * jax.random.uniform(seeds[7], (ROWS, TOP), jnp.float32) ** levels(seeds[7], (ROWS, TOP), ((0, 256),), -0.2, 0.2)), 0.05, 0.6)
    gate_weight = gaussian(seeds[8], (EXPERTS, D, FF), D ** -0.5, 0.0625, ((0, 32), (1, 8)))
    up_weight = gaussian(seeds[9], (EXPERTS, D, FF), D ** -0.5, 0.0625, ((0, 32), (1, 8)))
    down_weight = gaussian(seeds[10], (EXPERTS, FF, D), FF ** -0.5, 0.1875, ((0, 32), (2, 8)))
    return {"latent_cache": latent_cache, "old_slot": old_slot, "lengths": lengths, "new_latent": new_latent, "queries": queries, "hidden": hidden, "expert_ids": expert_ids, "expert_gates": expert_gates, "gate_weight": gate_weight, "up_weight": up_weight, "down_weight": down_weight}


score_scale = 0.07216878364870323


def attend_block(operands):
    key_rows, query_rows, length_rows = operands
    keys_wide = key_rows.astype(jnp.float32)
    query_wide = query_rows.reshape(-1, HEADS, KVW).astype(jnp.float32)
    scores = jnp.einsum("bhd,btd->bht", query_wide, keys_wide) * score_scale
    positions = jnp.arange(LEN, dtype=jnp.int32)
    valid = positions[None, None, :] <= length_rows[:, None, None]
    scores = jnp.where(valid, scores, -jnp.inf)
    top_score = jnp.max(scores, axis=2, keepdims=True)
    raised = jnp.exp(scores - top_score)
    weights = lax.optimization_barrier((raised / jnp.sum(raised, axis=2, keepdims=True)).astype(jnp.bfloat16))
    mixed = jnp.einsum("bht,btd->bhd", weights.astype(jnp.float32), keys_wide[:, :, :LAT])
    return mixed.astype(jnp.bfloat16).reshape(-1, HEADS * LAT)


def partial_sums(token_rows, weight):
    feature_part = D // N_REQ
    rows_wide = token_rows.reshape(-1, N_REQ, feature_part).astype(jnp.float32)
    weight_wide = weight.reshape(N_REQ, feature_part, -1).astype(jnp.float32)
    terms = jnp.einsum("rqd,qdf->qrf", rows_wide, weight_wide)
    terms = lax.optimization_barrier(terms.astype(jnp.bfloat16))
    return jnp.sum(terms.astype(jnp.float32), axis=0)


def run_expert(operands):
    token_rows, gate_one, up_one, down_one = operands
    gate_sum = partial_sums(token_rows, gate_one)
    up_sum = partial_sums(token_rows, up_one)
    units = (jax.nn.silu(gate_sum) * up_sum).astype(jnp.bfloat16)
    return jnp.dot(units, down_one, preferred_element_type=jnp.float32).astype(jnp.bfloat16)


def reference(latent_cache, old_slot, lengths, new_latent, queries, hidden, expert_ids, expert_gates, gate_weight, up_weight, down_weight):
    moved = jnp.take(latent_cache, old_slot, axis=0).reshape(ROWS, LEN, KVW)
    positions = jnp.arange(LEN, dtype=jnp.int32)
    at_length = positions[None, :] == lengths[:, None]
    cache_full = jnp.where(at_length[:, :, None], new_latent[:, None, :], moved)
    cache_out = cache_full.reshape(ROWS, LEN * KVW)
    block_count = ROWS // REQ_DEV
    attention = lax.map(attend_block, (cache_full.reshape(block_count, REQ_DEV, LEN, KVW), queries.reshape(block_count, REQ_DEV, HEADS * KVW), lengths.reshape(block_count, REQ_DEV)))
    attention = attention.reshape(ROWS, HEADS * LAT)

    device_count = N_REQ * N_EXP
    pair_count = REQ_DEV * TOP
    flat_ids = expert_ids.reshape(device_count, pair_count)
    onehot = (flat_ids[:, :, None] == jnp.arange(EXPERTS, dtype=jnp.int32)[None, None, :]).astype(jnp.int32)
    arrival_rank = jnp.sum((jnp.cumsum(onehot, axis=1) - 1) * onehot, axis=2).astype(jnp.int32)
    columns = jnp.arange(device_count, dtype=jnp.int32)[:, None] * CAP + arrival_rank
    sources = jnp.repeat(hidden.reshape(device_count, REQ_DEV, D), TOP, axis=1)
    buffers = jnp.zeros((EXPERTS, device_count * CAP, D), jnp.bfloat16).at[flat_ids, columns].set(sources)
    outputs = lax.map(run_expert, (buffers, gate_weight, up_weight, down_weight))
    picked = outputs[flat_ids, columns].reshape(ROWS, TOP, D).astype(jnp.float32)
    moe_out = jnp.sum(picked * expert_gates[:, :, None], axis=1).astype(jnp.bfloat16)
    return cache_out, attention, moe_out
```

```python
import functools

import jax
import jax.numpy as jnp
from jax import lax
from jax.experimental import pallas as pl
from jax.experimental.pallas import tpu as pltpu
from jax.sharding import PartitionSpec as P

LAT = 512
CAP = 3
CORES = 2
NOTE = 128

score_scale = 0.07216878364870323

VMEM = pl.BlockSpec(memory_space=pltpu.VMEM)
SMEM = pl.BlockSpec(memory_space=pltpu.SMEM)
PARAMS = pltpu.CompilerParams(vmem_limit_bytes=40 * 1024 * 1024)
BF = jnp.bfloat16
F32 = jnp.float32


def iota(shape, axis):
    return lax.broadcasted_iota(jnp.int32, shape, axis)


def dot(a, b, contract=((1,), (0,))):
    return lax.dot_general(a, b, (contract, ((), ())), preferred_element_type=F32)


def shape_of(shape, dtype=BF):
    return jax.ShapeDtypeStruct(shape, dtype)


def announce_kernel(column_span, slot_ref, hidden_ref, ids_ref, gates_ref, out_ref):
    peers, rows, width = out_ref.shape
    part = width - NOTE
    top = ids_ref.shape[1]
    lane = iota((rows, NOTE), 1)
    gates = gates_ref[...]
    first = gates.astype(BF).astype(F32)
    second = (gates - first).astype(BF).astype(F32)
    third = gates - first - second
    note = jnp.zeros((rows, NOTE), F32)
    for group, values in enumerate((ids_ref[...].astype(F32), first, second, third)):
        for k in range(top):
            note = jnp.where(lane == group * top + k, values[:, k : k + 1], note)
    for peer in range(peers):
        wanted = jnp.int32(0)
        for j in range(rows):
            slot = slot_ref[j]
            wanted += jnp.where(slot // column_span == peer, slot % rows, 0)
        own = jnp.where(lane == 4 * top, wanted.astype(F32), note)
        out_ref[peer, :, 0:part] = hidden_ref[:, peer * part : (peer + 1) * part]
        out_ref[peer, :, part:width] = own.astype(BF)


def route_kernel(top, arrived_ref, *refs):
    out_refs, weights_ref = refs[:-1], refs[-1]
    blocks, rows, width = arrived_ref.shape
    part = width - NOTE
    tokens = blocks * rows
    experts = out_refs[0].shape[0]
    stacked = jnp.concatenate([arrived_ref[b].astype(F32) for b in range(blocks)], axis=0)
    features = stacked[:, 0:part].astype(BF)
    note = stacked[:, part:width].T
    expert = iota((experts, tokens), 0).astype(F32)
    member = jnp.zeros((experts, tokens), F32)
    gate = jnp.zeros((experts, tokens), F32)
    for k in range(top):
        hit = note[k : k + 1, :] == expert
        value = note[top + k : top + k + 1, :] + note[2 * top + k : 2 * top + k + 1, :]
        value = value + note[3 * top + k : 3 * top + k + 1, :]
        member = jnp.where(hit, 1.0, member)
        gate = jnp.where(hit, value, gate)
    one, two = iota((tokens, tokens), 0), iota((tokens, tokens), 1)
    before = jnp.where((one // rows == two // rows) & (one < two), 1.0, 0.0).astype(BF)
    rank = dot(member.astype(BF), before)
    in_block = iota((blocks, tokens), 0) == iota((blocks, tokens), 1) // rows
    in_block = jnp.where(in_block, 1.0, 0.0)
    for c, out_ref in enumerate(out_refs):
        taken = jnp.where((member > 0.5) & (rank == float(c)), 1.0, 0.0)
        select = (taken[:, None, :] * in_block[None]).reshape(experts * blocks, tokens)
        weigh = ((taken * gate)[:, None, :] * in_block[None]).reshape(experts * blocks, tokens)
        out_ref[...] = dot(select.astype(BF), features).reshape(experts, blocks, part).astype(BF)
        high = weigh.astype(BF)
        weights_ref[c, 0] = high
        weights_ref[c, 1] = (weigh - high.astype(F32)).astype(BF)


def partial_kernel(place_ref, rows_ref, gate_ref, up_ref, send_ref, keep_ref):
    half = send_ref.shape[1]
    core = place_ref[1]
    keep_rows = rows_ref[pl.ds(pl.multiple_of(core * half, half), half), :]
    send_rows = rows_ref[pl.ds(pl.multiple_of((1 - core) * half, half), half), :]
    for which, weight_ref in enumerate((gate_ref, up_ref)):
        weight = weight_ref[...]
        send_ref[which] = dot(send_rows, weight).astype(BF)
        keep_ref[which] = dot(keep_rows, weight).astype(BF)


def pair_kernel(place_ref, keep_ref, got_ref, *out_refs):
    ring = len(out_refs)
    size = out_refs[0].shape[1]
    y = place_ref[0]
    for d, out_ref in enumerate(out_refs):
        start = pl.multiple_of(lax.rem(y + d, ring) * size, size)
        both = keep_ref[:, pl.ds(start, size), :].astype(F32)
        both += got_ref[:, pl.ds(start, size), :].astype(F32)
        out_ref[...] = both.astype(out_ref.dtype)


def units_kernel(own_ref, *refs):
    part_refs, out_ref = refs[:-1], refs[-1]
    total = own_ref[...]
    for part_ref in part_refs:
        total = total + part_ref[...].astype(F32)
    gate, up = total[0], total[1]
    out_ref[...] = (gate / (1.0 + jnp.exp(-gate)) * up).astype(BF)


def down_kernel(place_ref, *refs):
    ring = len(refs) - 3
    part_refs, other_ref, weight_ref, out_ref = refs[:ring], refs[-3], refs[-2], refs[-1]
    blocks = out_ref.shape[1]
    size = part_refs[0].shape[0]
    y, core = place_ref[0], place_ref[1]
    mine = jnp.concatenate([part_ref[...] for part_ref in part_refs], axis=0)
    for owner, rows in ((core, mine), (1 - core, other_ref[...])):
        result = dot(rows, weight_ref[...])
        for d in range(ring):
            start = owner * ring * (size // blocks) + lax.rem(y + d, ring) * (size // blocks)
            piece = result[d * size : (d + 1) * size].reshape(size // blocks, blocks, -1)
            out_ref[pl.ds(start, size // blocks)] = piece.astype(BF)


def combine_kernel(weights_ref, *refs):
    result_refs, out_ref = refs[:-1], refs[-1]
    total = 0.0
    for c, result_ref in enumerate(result_refs):
        experts, blocks, part = result_ref.shape
        results = result_ref[...].astype(F32).reshape(experts * blocks, part).astype(BF)
        for piece in range(2):
            total = total + dot(weights_ref[c, piece], results, ((0,), (0,)))
    out_ref[...] = total.reshape(out_ref.shape).astype(BF)


def spread_kernel(parts_ref, out_ref):
    peers, _, part = parts_ref.shape
    for peer in range(peers):
        out_ref[:, peer * part : (peer + 1) * part] = parts_ref[peer]


def stack_pairs(flat_ref, stacked_ref):
    rows = flat_ref.shape[0]
    total, span = stacked_ref.shape
    for p in range(0, total // rows, 2):
        both = [flat_ref[:, q * span : (q + 1) * span].astype(F32) for q in (p, p + 1)]
        stacked_ref[p * rows : (p + 2) * rows, :] = jnp.concatenate(both, axis=0).astype(BF)


def unstack_pairs(stacked, flat_ref):
    rows = flat_ref.shape[0]
    total, span = stacked.shape
    for p in range(total // rows):
        flat_ref[:, p * span : (p + 1) * span] = stacked[p * rows : (p + 1) * rows].astype(BF)


def pack_kernel(asked_ref, cache_ref, out_ref, stacked_ref):
    rows, pairs, span = out_ref.shape
    stack_pairs(cache_ref, stacked_ref)
    pair, column = iota((pairs, pairs * rows), 0), iota((pairs, pairs * rows), 1)
    same_pair = column // rows == pair
    select = [
        jnp.where(same_pair & (column % rows == asked_ref[r]), 1.0, 0.0) for r in range(rows)
    ]
    select = jnp.concatenate(select, axis=0).astype(BF)
    out_ref[...] = dot(select, stacked_ref[...]).reshape(rows, pairs, span).astype(BF)


def attend_kernel(
    source_ref, length_ref, arrived_ref, new_ref, queries_ref, cache_ref, mixed_ref,
    stacked_ref, keys_ref, out_ref,
):
    rows, pairs, span = arrived_ref.shape
    width = span // 2
    reach = -(-width // 128) * 128
    total = rows * pairs
    one, two = iota((total, total), 0), iota((total, total), 1)
    to_rows = (one // pairs == two % rows) & (one % pairs == two // rows)
    to_rows = jnp.where(to_rows, 1.0, 0.0).astype(BF)
    to_pairs = (one // rows == two % pairs) & (one % rows == two // pairs)
    to_pairs = jnp.where(to_pairs, 1.0, 0.0).astype(BF)
    stack_pairs(queries_ref, stacked_ref)
    queries = dot(to_rows, stacked_ref[...])
    turned = pltpu.roll(queries, width, 1)
    inside = iota((2 * pairs, reach), 1) < width
    pair, lane = iota((pairs, span), 0), iota((pairs, span), 1)
    column = iota((2 * pairs, 2 * pairs), 1)
    position = 2 * (column % pairs) + column // pairs
    for j in range(rows):
        length = length_ref[j]
        keys = arrived_ref[source_ref[j]].astype(F32)
        placed = (pair == length // 2) & ((lane >= width) == (length % 2 == 1))
        keys = jnp.where(placed, new_ref[j : j + 1, :], keys)
        keys_ref[j * pairs : (j + 1) * pairs, :] = keys.astype(BF)
        both = jnp.concatenate([keys, pltpu.roll(keys, width, 1)], axis=0)[:, 0:reach].astype(BF)
        own = slice(j * pairs, (j + 1) * pairs)
        heads = jnp.concatenate([queries[own, 0:reach], turned[own, 0:reach]], axis=0)
        heads = jnp.where(inside, heads, 0.0).astype(BF)
        scores = dot(heads, both, ((1,), (1,))) * score_scale
        scores = jnp.where(position <= length, scores, -jnp.inf)
        raised = jnp.exp(scores - jnp.max(scores, axis=1, keepdims=True))
        weights = (raised / jnp.sum(raised, axis=1, keepdims=True)).astype(BF)
        mixed = dot(weights, both[:, 0:LAT])
        mixed = jnp.concatenate([mixed[0:pairs], mixed[pairs:]], axis=1)
        out_ref[j * pairs : (j + 1) * pairs, :] = mixed.astype(BF)
    unstack_pairs(dot(to_pairs, keys_ref[...]), cache_ref)
    unstack_pairs(dot(to_pairs, out_ref[...]), mixed_ref)


def call(kernel, out_shape, in_specs, name, scratch=(), cost=None, **kw):
    return pl.pallas_call(
        kernel,
        out_shape=out_shape,
        in_specs=in_specs,
        out_specs=jax.tree.map(lambda _: VMEM, out_shape),
        scratch_shapes=list(scratch),
        compiler_params=PARAMS,
        cost_estimate=cost,
        name=name,
        **kw,
    )


def on_device(
    latent_cache,
    old_slot,
    lengths,
    new_latent,
    queries,
    hidden,
    expert_ids,
    expert_gates,
    gate_weight,
    up_weight,
    down_weight,
):
    rows, features = hidden.shape
    top = expert_ids.shape[1]
    peers = lax.axis_size("req")
    experts = lax.axis_size("exp")
    part = features // peers
    inner = gate_weight.shape[2]
    ring = peers // CORES
    me = lax.axis_index("req").astype(jnp.int32)
    place = jnp.stack([me // CORES, me % CORES])
    swap = [(k, k ^ 1) for k in range(peers)]

    def along(d):
        return [(k, (k + CORES * d) % peers) for k in range(peers)]

    column_span = experts * rows
    message = call(
        functools.partial(announce_kernel, column_span),
        shape_of((peers, rows, part + NOTE)),
        [SMEM, VMEM, VMEM, VMEM],
        "announce",
    )(old_slot, hidden, expert_ids, expert_gates)
    arrived = lax.all_to_all(message, "req", split_axis=0, concat_axis=0, tiled=True)

    *outgoing, weights = call(
        functools.partial(route_kernel, top),
        [shape_of((experts, peers, part))] * CAP + [shape_of((CAP, 2, experts * peers, peers * rows))],
        [VMEM],
        "route",
    )(arrived)

    width = new_latent.shape[1]
    span = 2 * width
    pairs = latent_cache.shape[1] // span
    asked = arrived[:, 0, part + 4 * top].astype(jnp.int32)
    packed = call(
        pack_kernel,
        shape_of((rows, pairs, span)),
        [SMEM, VMEM],
        "pack",
        [pltpu.VMEM((rows * pairs, span), BF)],
    )(asked, latent_cache)
    moved = lax.all_to_all(packed, "req", split_axis=0, concat_axis=0, tiled=True)

    slots = experts * peers
    half = slots // CORES
    size = half // ring
    gate_one, up_one, down_one = gate_weight[0], up_weight[0], down_weight[0]
    tile = min(inner, 512)
    returned = []
    for c in range(CAP):
        rows_here = lax.all_to_all(outgoing[c], "exp", split_axis=0, concat_axis=0, tiled=True)
        rows_here = rows_here.reshape(slots, part)
        send, keep = pl.pallas_call(
            partial_kernel,
            grid=(inner // tile,),
            out_shape=[shape_of((2, half, inner))] * 2,
            in_specs=[
                SMEM,
                pl.BlockSpec((slots, part), lambda i: (0, 0)),
                pl.BlockSpec((part, tile), lambda i: (0, i)),
                pl.BlockSpec((part, tile), lambda i: (0, i)),
            ],
            out_specs=[pl.BlockSpec((2, half, tile), lambda i: (0, 0, i))] * 2,
            compiler_params=PARAMS,
            name="partial",
        )(place, rows_here, gate_one, up_one)
        got = lax.ppermute(send, "req", swap)
        own, *sums = call(
            pair_kernel,
            [shape_of((2, size, inner), F32)] + [shape_of((2, size, inner))] * (ring - 1),
            [SMEM, VMEM, VMEM],
            "pair",
        )(place, keep, got)
        sums = [lax.ppermute(s, "req", along(d + 1)) for d, s in enumerate(sums)]
        units = call(
            units_kernel, shape_of((size, inner)), [VMEM] * ring, "units"
        )(own, *sums)
        gathered = [units] + [lax.ppermute(units, "req", along(-d)) for d in range(1, ring)]
        other = lax.ppermute(jnp.concatenate(gathered, axis=0), "req", swap)
        result = call(
            down_kernel,
            shape_of((experts, peers, part)),
            [SMEM] + [VMEM] * (ring + 2),
            "down",
        )(place, *gathered, other, down_one)
        returned.append(
            lax.all_to_all(result, "exp", split_axis=0, concat_axis=0, tiled=True)
        )

    combined = call(
        combine_kernel, shape_of((peers, rows, part)), [VMEM] * (CAP + 1), "combine"
    )(weights, *returned)
    parts = lax.all_to_all(combined, "req", split_axis=0, concat_axis=0, tiled=True)
    moe_out = call(spread_kernel, shape_of((rows, features)), [VMEM], "spread")(parts)

    new_pair = jnp.concatenate([new_latent, new_latent], axis=1).astype(F32)
    cache_out, attention = call(
        attend_kernel,
        [shape_of(latent_cache.shape), shape_of((rows, pairs * 2 * LAT))],
        [SMEM, SMEM, VMEM, VMEM, VMEM],
        "attend",
        [
            pltpu.VMEM((rows * pairs, span), BF),
            pltpu.VMEM((rows * pairs, span), BF),
            pltpu.VMEM((rows * pairs, 2 * LAT), BF),
        ],
    )(old_slot // column_span, lengths, moved, new_pair, queries)
    return (cache_out, attention, moe_out)


def solution(mesh):
    in_specs = (
        P(("req", "exp"), None),
        P(("req", "exp")),
        P(("req", "exp")),
        P(("req", "exp"), None),
        P(("req", "exp"), None),
        P(("req", "exp"), None),
        P(("req", "exp"), None),
        P(("req", "exp"), None),
        P("exp", "req", None),
        P("exp", "req", None),
        P("exp", None, "req"),
    )
    out_specs = (P(("req", "exp"), None), P(("req", "exp"), None), P(("req", "exp"), None))
    return jax.shard_map(
        on_device, mesh=mesh, in_specs=in_specs, out_specs=out_specs, check_vma=False
    )
```

```python
import functools

import jax
import jax.numpy as jnp
from jax import lax
from jax.experimental import pallas as pl
from jax.experimental.pallas import tpu as pltpu
from jax.sharding import PartitionSpec as P

LAT = 512
CAP = 3
CORES = 2
NOTE = 128
SEND = ((0, 1, 2),)
WORK = ((0, 1, 2),)

score_scale = 0.07216878364870323

VMEM = pl.BlockSpec(memory_space=pltpu.VMEM)
SMEM = pl.BlockSpec(memory_space=pltpu.SMEM)
PARAMS = pltpu.CompilerParams(vmem_limit_bytes=40 * 1024 * 1024)
BF = jnp.bfloat16
F32 = jnp.float32


def iota(shape, axis):
    return lax.broadcasted_iota(jnp.int32, shape, axis)


def dot(a, b, contract=((1,), (0,))):
    return lax.dot_general(a, b, (contract, ((), ())), preferred_element_type=F32)


def shape_of(shape, dtype=BF):
    return jax.ShapeDtypeStruct(shape, dtype)


def announce_kernel(column_span, slot_ref, hidden_ref, ids_ref, gates_ref, out_ref):
    peers, rows, width = out_ref.shape
    part = width - NOTE
    top = ids_ref.shape[1]
    lane = iota((rows, NOTE), 1)
    gates = gates_ref[...]
    first = gates.astype(BF).astype(F32)
    second = (gates - first).astype(BF).astype(F32)
    third = gates - first - second
    note = jnp.zeros((rows, NOTE), F32)
    for group, values in enumerate((ids_ref[...].astype(F32), first, second, third)):
        for k in range(top):
            note = jnp.where(lane == group * top + k, values[:, k : k + 1], note)
    for peer in range(peers):
        wanted = jnp.int32(0)
        for j in range(rows):
            slot = slot_ref[j]
            wanted += jnp.where(slot // column_span == peer, slot % rows, 0)
        own = jnp.where(lane == 4 * top, wanted.astype(F32), note)
        out_ref[peer, :, 0:part] = hidden_ref[:, peer * part : (peer + 1) * part]
        out_ref[peer, :, part:width] = own.astype(BF)


def route_kernel(top, groups, arrived_ref, *refs):
    out_refs, weights_refs = refs[: len(groups[0])], refs[len(groups[0]) :]
    blocks, rows, width = arrived_ref.shape
    part = width - NOTE
    tokens = blocks * rows
    experts = out_refs[0].shape[0]
    stacked = jnp.concatenate([arrived_ref[b].astype(F32) for b in range(blocks)], axis=0)
    features = stacked[:, 0:part].astype(BF)
    note = stacked[:, part:width].T
    expert = iota((experts, tokens), 0).astype(F32)
    member = jnp.zeros((experts, tokens), F32)
    gate = jnp.zeros((experts, tokens), F32)
    for k in range(top):
        hit = note[k : k + 1, :] == expert
        value = note[top + k : top + k + 1, :] + note[2 * top + k : 2 * top + k + 1, :]
        value = value + note[3 * top + k : 3 * top + k + 1, :]
        member = jnp.where(hit, 1.0, member)
        gate = jnp.where(hit, value, gate)
    one, two = iota((tokens, tokens), 0), iota((tokens, tokens), 1)
    before = jnp.where((one // rows == two // rows) & (one < two), 1.0, 0.0).astype(BF)
    rank = dot(member.astype(BF), before)
    in_block = iota((blocks, tokens), 0) == iota((blocks, tokens), 1) // rows
    in_block = jnp.where(in_block, 1.0, 0.0)
    taken = [jnp.where((member > 0.5) & (rank == float(c)), 1.0, 0.0) for c in range(CAP)]

    def slots_of(ranks, factor):
        pieces = [(taken[c] * factor)[:, None, :] * in_block[None] for c in ranks]
        both = jnp.concatenate(pieces, axis=1) if len(pieces) > 1 else pieces[0]
        return both.reshape(experts * len(ranks) * blocks, tokens)

    for ranks, out_ref in zip(groups[0], out_refs):
        select = slots_of(ranks, 1.0).astype(BF)
        out_ref[...] = dot(select, features).reshape(out_ref.shape).astype(BF)
    for ranks, weights_ref in zip(groups[1], weights_refs):
        weigh = slots_of(ranks, gate)
        high = weigh.astype(BF)
        weights_ref[0] = high
        weights_ref[1] = (weigh - high.astype(F32)).astype(BF)


def partial_kernel(other_core, low, place_ref, rows_ref, gate_ref, up_ref, *refs):
    out_ref = refs[-1]
    half = rows_ref.shape[0] // CORES
    part = rows_ref.shape[2]
    each = out_ref.shape[1] // half
    core = place_ref[1]
    core = 1 - core if other_core else core
    rows = rows_ref[pl.ds(core * half, half)].astype(F32)
    rows = rows[:, low : low + each, :].reshape(half * each, part).astype(BF)
    out_ref[0] = dot(rows, gate_ref[...]).astype(BF)
    out_ref[1] = dot(rows, up_ref[...]).astype(BF)


def pair_kernel(place_ref, keep_ref, got_ref, *out_refs):
    ring = len(out_refs)
    size = out_refs[0].shape[1]
    y = place_ref[0]
    for d, out_ref in enumerate(out_refs):
        start = pl.multiple_of(lax.rem(y + d, ring) * size, size)
        both = keep_ref[:, pl.ds(start, size), :].astype(F32)
        both += got_ref[:, pl.ds(start, size), :].astype(F32)
        out_ref[...] = both.astype(out_ref.dtype)


def units_kernel(own_ref, *refs):
    part_refs, out_ref = refs[:-1], refs[-1]
    total = own_ref[...]
    for part_ref in part_refs:
        total = total + part_ref[...].astype(F32)
    gate, up = total[0], total[1]
    out_ref[...] = (gate / (1.0 + jnp.exp(-gate)) * up).astype(BF)


def down_kernel(place_ref, *refs):
    ring = len(refs) - 3
    part_refs, other_ref, weight_ref, out_ref = refs[:ring], refs[-3], refs[-2], refs[-1]
    each = out_ref.shape[1]
    size = part_refs[0].shape[0]
    count = size // each
    y, core = place_ref[0], place_ref[1]
    mine = jnp.concatenate([part_ref[...] for part_ref in part_refs], axis=0)
    for owner, rows in ((core, mine), (1 - core, other_ref[...])):
        result = dot(rows, weight_ref[...])
        for d in range(ring):
            start = owner * ring * count + lax.rem(y + d, ring) * count
            piece = result[d * size : (d + 1) * size].reshape(count, each, -1)
            out_ref[pl.ds(start, count)] = piece.astype(BF)


def combine_kernel(*refs):
    count = len(refs) // 2
    weights_refs, result_refs, out_ref = refs[:count], refs[count:-1], refs[-1]
    total = 0.0
    for weights_ref, result_ref in zip(weights_refs, result_refs):
        experts, each, part = result_ref.shape
        results = result_ref[...].astype(F32).reshape(experts * each, part).astype(BF)
        for piece in range(2):
            total = total + dot(weights_ref[piece], results, ((0,), (0,)))
    out_ref[...] = total.reshape(out_ref.shape).astype(BF)


def spread_kernel(parts_ref, out_ref):
    peers, _, part = parts_ref.shape
    for peer in range(peers):
        out_ref[:, peer * part : (peer + 1) * part] = parts_ref[peer]


def stack_pairs(flat_ref, stacked_ref):
    rows = flat_ref.shape[0]
    total, span = stacked_ref.shape
    for p in range(0, total // rows, 2):
        both = [flat_ref[:, q * span : (q + 1) * span].astype(F32) for q in (p, p + 1)]
        stacked_ref[p * rows : (p + 2) * rows, :] = jnp.concatenate(both, axis=0).astype(BF)


def unstack_pairs(stacked, flat_ref):
    rows = flat_ref.shape[0]
    total, span = stacked.shape
    for p in range(total // rows):
        flat_ref[:, p * span : (p + 1) * span] = stacked[p * rows : (p + 1) * rows].astype(BF)


def pack_kernel(asked_ref, cache_ref, *refs):
    out_refs, stacked_ref = refs[:-1], refs[-1]
    rows = len(out_refs)
    pairs, span = out_refs[0].shape
    stack_pairs(cache_ref, stacked_ref)
    pair, column = iota((pairs, pairs * rows), 0), iota((pairs, pairs * rows), 1)
    same_pair = column // rows == pair
    select = [
        jnp.where(same_pair & (column % rows == asked_ref[r]), 1.0, 0.0) for r in range(rows)
    ]
    select = jnp.concatenate(select, axis=0).astype(BF)
    packed = dot(select, stacked_ref[...])
    for r, out_ref in enumerate(out_refs):
        out_ref[...] = packed[r * pairs : (r + 1) * pairs].astype(BF)


def attend_kernel(
    source_ref, length_ref, new_ref, queries_ref, *refs
):
    cache_ref, mixed_ref, arrived_ref, stacked_ref, keys_ref, out_ref = refs[-6:]
    rows, pairs, span = arrived_ref.shape
    for d, moved_ref in enumerate(refs[:-6]):
        arrived_ref[d] = moved_ref[...].astype(F32)
    width = span // 2
    reach = -(-width // 128) * 128
    total = rows * pairs
    one, two = iota((total, total), 0), iota((total, total), 1)
    to_rows = (one // pairs == two % rows) & (one % pairs == two // rows)
    to_rows = jnp.where(to_rows, 1.0, 0.0).astype(BF)
    to_pairs = (one // rows == two % pairs) & (one % rows == two // pairs)
    to_pairs = jnp.where(to_pairs, 1.0, 0.0).astype(BF)
    stack_pairs(queries_ref, stacked_ref)
    queries = dot(to_rows, stacked_ref[...])
    turned = pltpu.roll(queries, width, 1)
    inside = iota((2 * pairs, reach), 1) < width
    pair, lane = iota((pairs, span), 0), iota((pairs, span), 1)
    column = iota((2 * pairs, 2 * pairs), 1)
    position = 2 * (column % pairs) + column // pairs
    for j in range(rows):
        length = length_ref[j]
        keys = arrived_ref[source_ref[j]]
        placed = (pair == length // 2) & ((lane >= width) == (length % 2 == 1))
        keys = jnp.where(placed, new_ref[j : j + 1, :], keys)
        keys_ref[j * pairs : (j + 1) * pairs, :] = keys.astype(BF)
        both = jnp.concatenate([keys, pltpu.roll(keys, width, 1)], axis=0)[:, 0:reach].astype(BF)
        own = slice(j * pairs, (j + 1) * pairs)
        heads = jnp.concatenate([queries[own, 0:reach], turned[own, 0:reach]], axis=0)
        heads = jnp.where(inside, heads, 0.0).astype(BF)
        scores = dot(heads, both, ((1,), (1,))) * score_scale
        scores = jnp.where(position <= length, scores, -jnp.inf)
        raised = jnp.exp(scores - jnp.max(scores, axis=1, keepdims=True))
        weights = (raised / jnp.sum(raised, axis=1, keepdims=True)).astype(BF)
        mixed = dot(weights, both[:, 0:LAT])
        mixed = jnp.concatenate([mixed[0:pairs], mixed[pairs:]], axis=1)
        out_ref[j * pairs : (j + 1) * pairs, :] = mixed.astype(BF)
    unstack_pairs(dot(to_pairs, keys_ref[...]), cache_ref)
    unstack_pairs(dot(to_pairs, out_ref[...]), mixed_ref)


def call(kernel, out_shape, in_specs, name, scratch=(), cost=None, **kw):
    return pl.pallas_call(
        kernel,
        out_shape=out_shape,
        in_specs=in_specs,
        out_specs=jax.tree.map(lambda _: VMEM, out_shape),
        scratch_shapes=list(scratch),
        compiler_params=PARAMS,
        cost_estimate=cost,
        name=name,
        **kw,
    )


def on_device(
    latent_cache,
    old_slot,
    lengths,
    new_latent,
    queries,
    hidden,
    expert_ids,
    expert_gates,
    gate_weight,
    up_weight,
    down_weight,
):
    rows, features = hidden.shape
    top = expert_ids.shape[1]
    peers = lax.axis_size("req")
    experts = lax.axis_size("exp")
    part = features // peers
    inner = gate_weight.shape[2]
    ring = peers // CORES
    me = lax.axis_index("req").astype(jnp.int32)
    place = jnp.stack([me // CORES, me % CORES])
    swap = [(k, k ^ 1) for k in range(peers)]

    def along(d):
        return [(k, (k + CORES * d) % peers) for k in range(peers)]

    column_span = experts * rows
    message = call(
        functools.partial(announce_kernel, column_span),
        shape_of((peers, rows, part + NOTE)),
        [SMEM, VMEM, VMEM, VMEM],
        "announce",
    )(old_slot, hidden, expert_ids, expert_gates)
    arrived = lax.all_to_all(message, "req", split_axis=0, concat_axis=0, tiled=True)

    routed = call(
        functools.partial(route_kernel, top, (SEND, WORK)),
        [shape_of((experts, peers * len(g), part)) for g in SEND]
        + [shape_of((2, experts * peers * len(g), peers * rows)) for g in WORK],
        [VMEM],
        "route",
    )(arrived)
    outgoing, weights = routed[: len(SEND)], routed[len(SEND) :]

    width = new_latent.shape[1]
    span = 2 * width
    pairs = latent_cache.shape[1] // span
    asked = arrived[:, 0, part + 4 * top].astype(jnp.int32)
    asked = jnp.roll(asked, -me)
    packed = call(
        pack_kernel,
        [shape_of((pairs, span))] * peers,
        [SMEM, VMEM],
        "pack",
        [pltpu.VMEM((rows * pairs, span), BF)],
    )(asked, latent_cache)
    moved = [packed[0]] + [
        lax.ppermute(packed[d], "req", [(k, (k + d) % peers) for k in range(peers)])
        for d in range(1, peers)
    ]
    new_pair = jnp.concatenate([new_latent, new_latent], axis=1).astype(F32)
    source = lax.rem(me - old_slot // column_span + peers, peers)
    cache_out, attention = call(
        attend_kernel,
        [shape_of(latent_cache.shape), shape_of((rows, pairs * 2 * LAT))],
        [SMEM, SMEM, VMEM, VMEM] + [VMEM] * peers,
        "attend",
        [
            pltpu.VMEM((rows, pairs, span), F32),
            pltpu.VMEM((rows * pairs, span), BF),
            pltpu.VMEM((rows * pairs, span), BF),
            pltpu.VMEM((rows * pairs, 2 * LAT), BF),
        ],
    )(source, lengths, new_pair, queries, *moved)

    gate_one, up_one, down_one = gate_weight[0], up_weight[0], down_weight[0]
    tile = min(inner, 512)
    received = [
        lax.all_to_all(o, "exp", split_axis=0, concat_axis=0, tiled=True) for o in outgoing
    ]
    where_of = {c: (i, g.index(c) * peers) for i, g in enumerate(SEND) for c in g}

    def partial(other_core, group, after):
        i, low = where_of[group[0]]
        each = peers * len(group)
        half = experts // CORES * each
        return pl.pallas_call(
            functools.partial(partial_kernel, other_core, low),
            grid=(inner // tile,),
            out_shape=shape_of((2, half, inner)),
            in_specs=[
                SMEM,
                pl.BlockSpec(received[i].shape, lambda i: (0, 0, 0)),
                pl.BlockSpec((part, tile), lambda i: (0, i)),
                pl.BlockSpec((part, tile), lambda i: (0, i)),
            ]
            + [pl.BlockSpec(memory_space=pl.ANY)] * len(after),
            out_specs=pl.BlockSpec((2, half, tile), lambda i: (0, 0, i)),
            compiler_params=PARAMS,
            name="partial",
        )(place, received[i], gate_one, up_one, *after)

    returned = []
    for group in WORK:
        each = peers * len(group)
        size = experts // CORES * each // ring
        send = partial(True, group, [cache_out])
        got = lax.ppermute(send, "req", swap)
        keep = partial(False, group, [send])
        own, *sums = call(
            pair_kernel,
            [shape_of((2, size, inner), F32)] + [shape_of((2, size, inner))] * (ring - 1),
            [SMEM, VMEM, VMEM],
            "pair",
        )(place, keep, got)
        sums = [lax.ppermute(s, "req", along(d + 1)) for d, s in enumerate(sums)]
        units = call(units_kernel, shape_of((size, inner)), [VMEM] * ring, "units")(own, *sums)
        gathered = [units] + [lax.ppermute(units, "req", along(-d)) for d in range(1, ring)]
        other = lax.ppermute(jnp.concatenate(gathered, axis=0), "req", swap)
        result = call(
            down_kernel,
            shape_of((experts, each, part)),
            [SMEM] + [VMEM] * (ring + 2),
            "down",
        )(place, *gathered, other, down_one)
        returned.append(lax.all_to_all(result, "exp", split_axis=0, concat_axis=0, tiled=True))

    combined = call(
        combine_kernel, shape_of((peers, rows, part)), [VMEM] * (2 * len(WORK)), "combine"
    )(*weights, *returned)
    parts = lax.all_to_all(combined, "req", split_axis=0, concat_axis=0, tiled=True)
    moe_out = call(spread_kernel, shape_of((rows, features)), [VMEM], "spread")(parts)
    return (cache_out, attention, moe_out)


def solution(mesh):
    in_specs = (
        P(("req", "exp"), None),
        P(("req", "exp")),
        P(("req", "exp")),
        P(("req", "exp"), None),
        P(("req", "exp"), None),
        P(("req", "exp"), None),
        P(("req", "exp"), None),
        P(("req", "exp"), None),
        P("exp", "req", None),
        P("exp", "req", None),
        P("exp", None, "req"),
    )
    out_specs = (P(("req", "exp"), None), P(("req", "exp"), None), P(("req", "exp"), None))
    return jax.shard_map(
        on_device, mesh=mesh, in_specs=in_specs, out_specs=out_specs, check_vma=False
    )
```

```python
import functools

import jax
import jax.numpy as jnp
from jax import lax
from jax.experimental import pallas as pl
from jax.experimental.pallas import tpu as pltpu
from jax.sharding import PartitionSpec as P

LAT = 512
CAP = 3
CORES = 2
NOTE = 128
ROUTE, PART, DOWN, TILES = 32, 58, 32, 2

score_scale = 0.07216878364870323

VMEM = pl.BlockSpec(memory_space=pltpu.VMEM)
SMEM = pl.BlockSpec(memory_space=pltpu.SMEM)
ANY = pl.BlockSpec(memory_space=pl.ANY)
MIB = 1024 * 1024
BF = jnp.bfloat16
F32 = jnp.float32


def iota(shape, axis):
    return lax.broadcasted_iota(jnp.int32, shape, axis)


def dot(a, b, contract=((1,), (0,))):
    return lax.dot_general(a, b, (contract, ((), ())), preferred_element_type=F32)


def shape_of(shape, dtype=BF):
    return jax.ShapeDtypeStruct(shape, dtype)


def announce_kernel(column_span, *refs):
    sources, out_ref, targets, sems = refs[:4], refs[4], refs[5:9], refs[9]
    copies = [pltpu.make_async_copy(a, b, sems.at[i]) for i, (a, b) in enumerate(zip(sources, targets))]
    for copy in copies:
        copy.start()
    for copy in copies:
        copy.wait()
    slot_ref, hidden_ref, ids_ref, gates_ref = targets
    ring, rows, width = out_ref.shape
    part = width - NOTE
    top = ids_ref.shape[1]
    lane = iota((rows, NOTE), 1)
    gates = gates_ref[...]
    first = gates.astype(BF).astype(F32)
    second = (gates - first).astype(BF).astype(F32)
    third = gates - first - second
    note = jnp.zeros((rows, NOTE), F32)
    for group, values in enumerate((ids_ref[...].astype(F32), first, second, third)):
        for k in range(top):
            note = jnp.where(lane == group * top + k, values[:, k : k + 1], note)
    for chip in range(ring):
        own = note
        for core in range(CORES):
            wanted = jnp.int32(0)
            for j in range(rows):
                slot = slot_ref[j]
                same = slot // column_span == chip * CORES + core
                wanted += jnp.where(same, slot % rows, 0)
            own = jnp.where(lane == 4 * top + core, wanted.astype(F32), own)
        out_ref[chip, :, 0:part] = hidden_ref[:, chip * part : (chip + 1) * part]
        out_ref[chip, :, part:width] = own.astype(BF)


def routing(top, experts, arrived_ref):
    blocks, rows, width = arrived_ref.shape
    tokens = blocks * rows
    stacked = jnp.concatenate([arrived_ref[b].astype(F32) for b in range(blocks)], axis=0)
    note = stacked[:, width - NOTE : width]
    note = jnp.concatenate([note, jnp.zeros((NOTE - tokens, NOTE), F32)], axis=0).T[:, 0:tokens]
    expert = iota((experts, tokens), 0).astype(F32)
    member = jnp.zeros((experts, tokens), F32)
    gate = jnp.zeros((experts, tokens), F32)
    for k in range(top):
        hit = note[k : k + 1, :] == expert
        value = note[top + k : top + k + 1, :] + note[2 * top + k : 2 * top + k + 1, :]
        value = value + note[3 * top + k : 3 * top + k + 1, :]
        member = jnp.where(hit, 1.0, member)
        gate = jnp.where(hit, value, gate)
    one, two = iota((tokens, tokens), 0), iota((tokens, tokens), 1)
    before = jnp.where((one // rows == two // rows) & (one < two), 1.0, 0.0).astype(BF)
    rank = dot(member.astype(BF), before)
    place = rank * blocks + (iota((experts, tokens), 1) // rows).astype(F32)
    place = jnp.where(member > 0.5, place, -1.0)
    slots = CAP * blocks
    row = iota((experts, CORES * slots, tokens), 1)

    def slots_of(half, factor):
        wanted = jnp.where(row // slots == half, row % slots, -2).astype(F32)
        taken = jnp.where(wanted == place[:, None, :], factor, 0.0)
        return taken.reshape(experts * CORES * slots, tokens)

    return stacked[:, 0 : width - NOTE].astype(BF), gate[:, None, :], slots_of


def route_kernel(top, arrived_ref, out_ref):
    features, _, slots_of = routing(top, out_ref.shape[0], arrived_ref)
    part = features.shape[1] // CORES
    total = 0.0
    for half in range(CORES):
        own = features[:, half * part : (half + 1) * part]
        total = total + dot(slots_of(half, 1.0).astype(BF), own)
    out_ref[...] = total.reshape(out_ref.shape).astype(BF)


def weigh_kernel(top, experts, arrived_ref, out_ref):
    _, gate, slots_of = routing(top, experts, arrived_ref)
    weigh = [slots_of(half, gate) for half in range(CORES)]
    high = [w.astype(BF).astype(F32) for w in weigh]
    low = [w - h for w, h in zip(weigh, high)]
    out_ref[...] = jnp.concatenate(high + low, axis=1).astype(BF)


def half_select(core, count, slots):
    size = count * slots
    row = iota((CORES * size, 1), 0)
    half = jnp.where(row < size, core, 1 - core)
    target = (row % size) // slots * CORES * slots + half * slots + row % slots
    column = iota((CORES * size, CORES * size), 1)
    return jnp.where(column == target, 1.0, 0.0).astype(BF)


def write_sums(own_ref, other_ref, weight_ref, weight2_ref, out_refs):
    size = out_refs[0].shape[0]
    result = dot(own_ref[...], weight_ref[...]) + dot(other_ref[...], weight2_ref[...])
    for d, out_ref in enumerate(out_refs):
        out_ref[...] = result[d * size : (d + 1) * size].astype(out_ref.dtype)


def gate_kernel(place_ref, rows_ref, gate_ref, gate2_ref, *refs):
    own_ref, other_ref, out_refs = refs[0], refs[1], refs[2:]
    ring, size = len(out_refs), out_refs[0].shape[0]
    sources, double, part = rows_ref.shape
    count = sources // ring

    @pl.when(pl.program_id(0) == 0)
    def _():
        select = half_select(place_ref[1], count, double // CORES)
        for d in range(ring):
            start = lax.rem(place_ref[0] + d, ring) * count
            rows = rows_ref[pl.ds(start, count)].astype(F32)
            both = dot(select, rows.reshape(count * double, part).astype(BF)).astype(BF)
            own_ref[d * size : (d + 1) * size, :] = both[0:size]
            other_ref[d * size : (d + 1) * size, :] = both[size:]

    write_sums(own_ref, other_ref, gate_ref, gate2_ref, out_refs)


def up_kernel(own_ref, other_ref, up_ref, up2_ref, *out_refs):
    write_sums(own_ref, other_ref, up_ref, up2_ref, out_refs)


def units_kernel(*refs):
    part_refs, out_ref = refs[:-1], refs[-1]
    gate, up = (sum(ref[...].astype(F32) for ref in part_refs[i::2]) for i in range(2))
    units = (gate / (1.0 + jnp.exp(-gate)) * up).astype(BF)
    for d in range(out_ref.shape[0]):
        out_ref[d] = units


def down_kernel(place_ref, units_ref, weight_ref, weight2_ref, out_ref):
    ring, size, inner = units_ref.shape
    sources, double, part = out_ref.shape
    count = sources // ring
    rows = jnp.concatenate([units_ref[d] for d in range(ring)], axis=0)
    own = dot(rows, weight_ref[...]).astype(BF)
    other = dot(rows, weight2_ref[...]).astype(BF)
    select = half_select(place_ref[1], count, double // CORES)
    for d in range(ring):
        piece = slice(d * size, (d + 1) * size)
        both = dot(select, jnp.concatenate([own[piece], other[piece]], axis=0), ((0,), (0,)))
        out_ref[d * count : (d + 1) * count] = both.reshape(count, double, part).astype(BF)


def combine_kernel(weights_ref, result_ref, out_ref):
    experts, double, part = result_ref.shape
    ring, rows, _ = out_ref.shape
    results = result_ref[...].astype(F32).reshape(experts * double, part).astype(BF)
    sums = dot(weights_ref[...], results, ((0,), (0,)))
    tokens = ring * rows
    for half in range(CORES):
        total = sums[half * tokens : (half + 1) * tokens]
        total = total + sums[(CORES + half) * tokens : (CORES + half + 1) * tokens]
        out_ref[:, :, half * part : (half + 1) * part] = total.reshape(ring, rows, part).astype(BF)


def spread_kernel(parts_ref, out_ref):
    peers, _, part = parts_ref.shape
    for peer in range(peers):
        out_ref[:, peer * part : (peer + 1) * part] = parts_ref[peer]


def stack_pairs(flat_ref, stacked_ref):
    rows = flat_ref.shape[0]
    total, span = stacked_ref.shape
    for p in range(0, total // rows, 2):
        both = [flat_ref[:, q * span : (q + 1) * span].astype(F32) for q in (p, p + 1)]
        stacked_ref[p * rows : (p + 2) * rows, :] = jnp.concatenate(both, axis=0).astype(BF)


def unstack_pairs(stacked, flat_ref):
    rows = flat_ref.shape[0]
    total, span = stacked.shape
    for p in range(total // rows):
        flat_ref[:, p * span : (p + 1) * span] = stacked[p * rows : (p + 1) * rows].astype(BF)


def pack_kernel(asked_ref, cache_ref, *refs):
    out_refs, stacked_ref = refs[:-1], refs[-1]
    rows = len(out_refs)
    pairs, span = out_refs[0].shape
    stack_pairs(cache_ref, stacked_ref)
    pair, column = iota((pairs, pairs * rows), 0), iota((pairs, pairs * rows), 1)
    same_pair = column // rows == pair
    select = [
        jnp.where(same_pair & (column % rows == asked_ref[r]), 1.0, 0.0) for r in range(rows)
    ]
    select = jnp.concatenate(select, axis=0).astype(BF)
    packed = dot(select, stacked_ref[...])
    for r, out_ref in enumerate(out_refs):
        out_ref[...] = packed[r * pairs : (r + 1) * pairs].astype(BF)


def attend_kernel(
    source_ref, length_ref, new_ref, queries_ref, *refs
):
    cache_ref, mixed_ref, token_ref, arrived_ref, stacked_ref, keys_ref, out_ref = refs[-7:]
    token_ref[...] = jnp.zeros(token_ref.shape, F32)
    rows, pairs, span = arrived_ref.shape
    for d, moved_ref in enumerate(refs[:-7]):
        arrived_ref[d] = moved_ref[...].astype(F32)
    width = span // 2
    reach = -(-width // 128) * 128
    total = rows * pairs
    one, two = iota((total, total), 0), iota((total, total), 1)
    to_rows = (one // pairs == two % rows) & (one % pairs == two // rows)
    to_rows = jnp.where(to_rows, 1.0, 0.0).astype(BF)
    to_pairs = (one // rows == two % pairs) & (one % rows == two // pairs)
    to_pairs = jnp.where(to_pairs, 1.0, 0.0).astype(BF)
    stack_pairs(queries_ref, stacked_ref)
    queries = dot(to_rows, stacked_ref[...])
    turned = pltpu.roll(queries, width, 1)
    inside = iota((2 * pairs, reach), 1) < width
    pair, lane = iota((pairs, span), 0), iota((pairs, span), 1)
    column = iota((2 * pairs, 2 * pairs), 1)
    position = 2 * (column % pairs) + column // pairs
    for j in range(rows):
        length = length_ref[j]
        keys = arrived_ref[source_ref[j]]
        placed = (pair == length // 2) & ((lane >= width) == (length % 2 == 1))
        keys = jnp.where(placed, new_ref[j : j + 1, :], keys)
        keys_ref[j * pairs : (j + 1) * pairs, :] = keys.astype(BF)
        both = jnp.concatenate([keys, pltpu.roll(keys, width, 1)], axis=0)[:, 0:reach].astype(BF)
        own = slice(j * pairs, (j + 1) * pairs)
        heads = jnp.concatenate([queries[own, 0:reach], turned[own, 0:reach]], axis=0)
        heads = jnp.where(inside, heads, 0.0).astype(BF)
        scores = dot(heads, both, ((1,), (1,))) * score_scale
        scores = jnp.where(position <= length, scores, -jnp.inf)
        raised = jnp.exp(scores - jnp.max(scores, axis=1, keepdims=True))
        weights = (raised / jnp.sum(raised, axis=1, keepdims=True)).astype(BF)
        mixed = dot(weights, both[:, 0:LAT])
        mixed = jnp.concatenate([mixed[0:pairs], mixed[pairs:]], axis=1)
        out_ref[j * pairs : (j + 1) * pairs, :] = mixed.astype(BF)
    unstack_pairs(dot(to_pairs, keys_ref[...]), cache_ref)
    unstack_pairs(dot(to_pairs, out_ref[...]), mixed_ref)


def call(kernel, out_shape, in_specs, name, scratch=(), after=(), limit=32):
    count = len(in_specs)

    def body(*refs):
        kernel(*refs[:count], *refs[count + len(after) :])

    return lambda *args: pl.pallas_call(
        body,
        out_shape=out_shape,
        in_specs=in_specs + [VMEM] * len(after),
        out_specs=jax.tree.map(lambda _: VMEM, out_shape),
        scratch_shapes=list(scratch),
        compiler_params=pltpu.CompilerParams(vmem_limit_bytes=limit * MIB),
        name=name,
    )(*args, *after)


TOKEN = jax.ShapeDtypeStruct((8, 128), F32)


def on_device(
    latent_cache,
    old_slot,
    lengths,
    new_latent,
    queries,
    hidden,
    expert_ids,
    expert_gates,
    gate_weight,
    up_weight,
    down_weight,
):
    rows, features = hidden.shape
    top = expert_ids.shape[1]
    peers = lax.axis_size("req")
    experts = lax.axis_size("exp")
    ring = peers // CORES
    part = features // ring
    inner = gate_weight.shape[2]
    me = lax.axis_index("req").astype(jnp.int32)
    place = jnp.stack([me // CORES, me % CORES])
    swap = [(k, k ^ 1) for k in range(peers)]
    same_core = [[k for k in range(peers) if k % CORES == c] for c in range(CORES)]

    def along(d):
        return [(k, (k + CORES * d) % peers) for k in range(peers)]

    def exchange_y(x):
        return lax.all_to_all(
            x, "req", split_axis=0, concat_axis=0, tiled=True, axis_index_groups=same_core
        )

    column_span = experts * rows
    message = call(
        functools.partial(announce_kernel, column_span),
        shape_of((ring, rows, part + NOTE)),
        [ANY] * 4,
        "announce",
        [
            pltpu.SMEM(old_slot.shape, jnp.int32),
            pltpu.VMEM(hidden.shape, BF),
            pltpu.VMEM(expert_ids.shape, jnp.int32),
            pltpu.VMEM(expert_gates.shape, F32),
            pltpu.SemaphoreType.DMA((4,)),
        ],
        limit=56,
    )(old_slot, hidden, expert_ids, expert_gates)
    arrived = exchange_y(message)

    own_weights = [w[0] for w in (gate_weight, up_weight, down_weight)]
    sibling_weights = [lax.ppermute(w, "req", swap) for w in own_weights]

    width = new_latent.shape[1]
    span = 2 * width
    pairs = latent_cache.shape[1] // span
    asked = arrived[:, 0, part + 4 * top : part + 4 * top + CORES].astype(jnp.int32)
    asked = asked.T
    core = place[1]
    other = lax.ppermute(lax.dynamic_index_in_dim(asked, 1 - core, 0, False), "req", swap)
    asked = lax.dynamic_index_in_dim(asked, core, 0, False)
    asked = jnp.where(core == 0, jnp.stack([asked, other], 1), jnp.stack([other, asked], 1))
    asked = jnp.roll(asked.reshape(-1), -me)
    packed = call(
        pack_kernel,
        [shape_of((pairs, span))] * peers,
        [SMEM, VMEM],
        "pack",
        [pltpu.VMEM((rows * pairs, span), BF)],
    )(asked, latent_cache)
    moved = [packed[0]] + [
        lax.ppermute(packed[d], "req", [(k, (k + d) % peers) for k in range(peers)])
        for d in range(1, peers)
    ]
    new_pair = jnp.concatenate([new_latent, new_latent], axis=1).astype(F32)
    source = lax.rem(me - old_slot // column_span + peers, peers)
    cache_out, attention, done = call(
        attend_kernel,
        [shape_of(latent_cache.shape), shape_of((rows, pairs * 2 * LAT)), TOKEN],
        [SMEM, SMEM, VMEM, VMEM] + [VMEM] * peers,
        "attend",
        [
            pltpu.VMEM((rows, pairs, span), F32),
            pltpu.VMEM((rows * pairs, span), BF),
            pltpu.VMEM((rows * pairs, span), BF),
            pltpu.VMEM((rows * pairs, 2 * LAT), BF),
        ],
    )(source, lengths, new_pair, queries, *moved)


    slots = CAP * ring
    outgoing = call(
        functools.partial(route_kernel, top),
        shape_of((experts, CORES * slots, part // CORES)),
        [VMEM],
        "route",
        limit=ROUTE,
    )(arrived)
    received = lax.all_to_all(outgoing, "exp", split_axis=0, concat_axis=0, tiled=True)
    weights = call(
        functools.partial(weigh_kernel, top, experts),
        shape_of((experts * CORES * slots, 2 * CORES * ring * rows)),
        [VMEM],
        "weigh",
    )(arrived)

    size = experts // ring * slots
    tile = inner // TILES
    width_own = part // CORES
    column = pl.BlockSpec((width_own, tile), lambda i: (0, i))
    sums_spec = [pl.BlockSpec((size, tile), lambda i: (0, i))] * ring
    sums_shape = [shape_of((size, inner), F32)] + [shape_of((size, inner))] * (ring - 1)
    rows_spec = [pl.BlockSpec((ring * size, width_own), lambda i: (0, 0))] * 2
    params = pltpu.CompilerParams(vmem_limit_bytes=PART * MIB)
    mine, theirs, *gates = pl.pallas_call(
        lambda *refs: gate_kernel(*refs[:4], *refs[6:]),
        grid=(TILES,),
        out_shape=[shape_of((ring * size, width_own))] * 2 + sums_shape,
        in_specs=[SMEM, pl.BlockSpec(received.shape, lambda i: (0, 0, 0))] + [column] * 2 + [ANY] * 2,
        out_specs=rows_spec + sums_spec,
        compiler_params=params,
        name="gate",
    )(place, received, own_weights[0], sibling_weights[0], done, weights)
    ups = pl.pallas_call(
        up_kernel,
        grid=(TILES,),
        out_shape=sums_shape,
        in_specs=rows_spec + [column] * 2,
        out_specs=sums_spec,
        compiler_params=params,
        name="up",
    )(mine, theirs, own_weights[1], sibling_weights[1])
    sent = [gates[0], ups[0]]
    for d in range(1, ring):
        sent += [lax.ppermute(x[d], "req", along(d)) for x in (gates, ups)]
    units = call(units_kernel, shape_of((ring, size, inner)), [VMEM] * (2 * ring), "units")(*sent)
    result = call(
        down_kernel,
        shape_of(received.shape),
        [SMEM] + [VMEM] * 3,
        "down",
        limit=DOWN,
    )(place, exchange_y(units), own_weights[2], sibling_weights[2])
    returned = lax.all_to_all(result, "exp", split_axis=0, concat_axis=0, tiled=True)
    combined = call(combine_kernel, shape_of((ring, rows, part)), [VMEM] * 2, "combine")(
        weights, returned
    )
    moe_out = call(spread_kernel, shape_of((rows, features)), [VMEM], "spread")(
        exchange_y(combined)
    )

    return (cache_out, attention, moe_out)


def solution(mesh):
    in_specs = (
        P(("req", "exp"), None),
        P(("req", "exp")),
        P(("req", "exp")),
        P(("req", "exp"), None),
        P(("req", "exp"), None),
        P(("req", "exp"), None),
        P(("req", "exp"), None),
        P(("req", "exp"), None),
        P("exp", "req", None),
        P("exp", "req", None),
        P("exp", None, "req"),
    )
    out_specs = (P(("req", "exp"), None), P(("req", "exp"), None), P(("req", "exp"), None))
    return jax.shard_map(
        on_device, mesh=mesh, in_specs=in_specs, out_specs=out_specs, check_vma=False
    )
```

```python
import functools

import jax
import jax.numpy as jnp
from jax import lax
from jax.experimental import pallas as pl
from jax.experimental.pallas import tpu as pltpu
from jax.sharding import PartitionSpec as P

LAT = 512
CAP = 3
CORES = 2
NOTE = 128
ROUTE, PART, DOWN, TILES = 32, 58, 32, 2

score_scale = 0.07216878364870323

VMEM = pl.BlockSpec(memory_space=pltpu.VMEM)
SMEM = pl.BlockSpec(memory_space=pltpu.SMEM)
ANY = pl.BlockSpec(memory_space=pl.ANY)
MIB = 1024 * 1024
BF = jnp.bfloat16
F32 = jnp.float32


def iota(shape, axis):
    return lax.broadcasted_iota(jnp.int32, shape, axis)


def dot(a, b, contract=((1,), (0,))):
    return lax.dot_general(a, b, (contract, ((), ())), preferred_element_type=F32)


def shape_of(shape, dtype=BF):
    return jax.ShapeDtypeStruct(shape, dtype)


def announce_kernel(column_span, *refs):
    sources, out_ref, targets, sems = refs[:4], refs[4], refs[5:9], refs[9]
    copies = [pltpu.make_async_copy(a, b, sems.at[i]) for i, (a, b) in enumerate(zip(sources, targets))]
    for copy in copies:
        copy.start()
    for copy in copies:
        copy.wait()
    slot_ref, hidden_ref, ids_ref, gates_ref = targets
    ring, rows, width = out_ref.shape
    part = width - NOTE
    top = ids_ref.shape[1]
    lane = iota((rows, NOTE), 1)
    gates = gates_ref[...]
    first = gates.astype(BF).astype(F32)
    second = (gates - first).astype(BF).astype(F32)
    third = gates - first - second
    note = jnp.zeros((rows, NOTE), F32)
    for group, values in enumerate((ids_ref[...].astype(F32), first, second, third)):
        for k in range(top):
            note = jnp.where(lane == group * top + k, values[:, k : k + 1], note)
    for chip in range(ring):
        own = note
        for core in range(CORES):
            wanted = jnp.int32(0)
            for j in range(rows):
                slot = slot_ref[j]
                same = slot // column_span == chip * CORES + core
                wanted += jnp.where(same, slot % rows, 0)
            own = jnp.where(lane == 4 * top + core, wanted.astype(F32), own)
        out_ref[chip, :, 0:part] = hidden_ref[:, chip * part : (chip + 1) * part]
        out_ref[chip, :, part:width] = own.astype(BF)


def routing(top, experts, arrived_ref):
    blocks, rows, width = arrived_ref.shape
    tokens = blocks * rows
    stacked = jnp.concatenate([arrived_ref[b].astype(F32) for b in range(blocks)], axis=0)
    note = stacked[:, width - NOTE : width]
    note = jnp.concatenate([note, jnp.zeros((NOTE - tokens, NOTE), F32)], axis=0).T[:, 0:tokens]
    expert = iota((experts, tokens), 0).astype(F32)
    member = jnp.zeros((experts, tokens), F32)
    gate = jnp.zeros((experts, tokens), F32)
    for k in range(top):
        hit = note[k : k + 1, :] == expert
        value = note[top + k : top + k + 1, :] + note[2 * top + k : 2 * top + k + 1, :]
        value = value + note[3 * top + k : 3 * top + k + 1, :]
        member = jnp.where(hit, 1.0, member)
        gate = jnp.where(hit, value, gate)
    one, two = iota((tokens, tokens), 0), iota((tokens, tokens), 1)
    before = jnp.where((one // rows == two // rows) & (one < two), 1.0, 0.0).astype(BF)
    rank = dot(member.astype(BF), before)
    place = rank * blocks + (iota((experts, tokens), 1) // rows).astype(F32)
    place = jnp.where(member > 0.5, place, -1.0)
    slots = CAP * blocks
    row = iota((1, CORES * slots, tokens), 1)

    def slots_of(half, factor):
        wanted = jnp.where(row // slots == half, row % slots, -2).astype(F32)
        taken = jnp.where(wanted == place[:, None, :], factor, 0.0)
        return taken.reshape(experts * CORES * slots, tokens)

    return stacked[:, 0 : width - NOTE].astype(BF), gate[:, None, :], slots_of


def route_kernel(top, arrived_ref, out_ref):
    features, _, slots_of = routing(top, out_ref.shape[0], arrived_ref)
    part = features.shape[1] // CORES
    total = 0.0
    for half in range(CORES):
        own = features[:, half * part : (half + 1) * part]
        total = total + dot(slots_of(half, 1.0).astype(BF), own)
    out_ref[...] = total.reshape(out_ref.shape).astype(BF)


def weigh_kernel(top, experts, arrived_ref, out_ref):
    _, gate, slots_of = routing(top, experts, arrived_ref)
    weigh = [slots_of(half, gate) for half in range(CORES)]
    high = [w.astype(BF).astype(F32) for w in weigh]
    low = [w - h for w, h in zip(weigh, high)]
    out_ref[...] = jnp.concatenate(high + low, axis=1).astype(BF)


def half_select(core, count, slots):
    size = count * slots
    row = iota((CORES * size, 1), 0)
    half = jnp.where(row < size, core, 1 - core)
    target = (row % size) // slots * CORES * slots + half * slots + row % slots
    column = iota((CORES * size, CORES * size), 1)
    return jnp.where(column == target, 1.0, 0.0).astype(BF)


def write_sums(own_ref, other_ref, weight_ref, weight2_ref, out_refs):
    size = out_refs[0].shape[0]
    result = dot(own_ref[...], weight_ref[...]) + dot(other_ref[...], weight2_ref[...])
    for d, out_ref in enumerate(out_refs):
        out_ref[...] = result[d * size : (d + 1) * size].astype(out_ref.dtype)


def gate_kernel(place_ref, rows_ref, gate_ref, gate2_ref, *refs):
    own_ref, other_ref, out_refs = refs[0], refs[1], refs[2:]
    ring, size = len(out_refs), out_refs[0].shape[0]
    sources, double, part = rows_ref.shape
    count = sources // ring

    @pl.when(pl.program_id(0) == 0)
    def _():
        select = half_select(place_ref[1], count, double // CORES)
        for d in range(ring):
            start = lax.rem(place_ref[0] + d, ring) * count
            rows = rows_ref[pl.ds(start, count)].astype(F32)
            both = dot(select, rows.reshape(count * double, part).astype(BF)).astype(BF)
            own_ref[d * size : (d + 1) * size, :] = both[0:size]
            other_ref[d * size : (d + 1) * size, :] = both[size:]

    write_sums(own_ref, other_ref, gate_ref, gate2_ref, out_refs)


def up_kernel(own_ref, other_ref, up_ref, up2_ref, *out_refs):
    write_sums(own_ref, other_ref, up_ref, up2_ref, out_refs)


def units_kernel(*refs):
    part_refs, out_ref = refs[:-1], refs[-1]
    gate, up = (sum(ref[...].astype(F32) for ref in part_refs[i::2]) for i in range(2))
    units = (gate / (1.0 + jnp.exp(-gate)) * up).astype(BF)
    for d in range(out_ref.shape[0]):
        out_ref[d] = units


def down_kernel(place_ref, units_ref, weight_ref, weight2_ref, out_ref):
    ring, size, inner = units_ref.shape
    sources, double, part = out_ref.shape
    count = sources // ring
    rows = jnp.concatenate([units_ref[d] for d in range(ring)], axis=0)
    own = dot(rows, weight_ref[...]).astype(BF)
    other = dot(rows, weight2_ref[...]).astype(BF)
    select = half_select(place_ref[1], count, double // CORES)
    for d in range(ring):
        piece = slice(d * size, (d + 1) * size)
        both = dot(select, jnp.concatenate([own[piece], other[piece]], axis=0), ((0,), (0,)))
        out_ref[d * count : (d + 1) * count] = both.reshape(count, double, part).astype(BF)


def combine_kernel(weights_ref, result_ref, out_ref):
    experts, double, part = result_ref.shape
    ring, rows, _ = out_ref.shape
    results = result_ref[...].astype(F32).reshape(experts * double, part).astype(BF)
    sums = dot(weights_ref[...], results, ((0,), (0,)))
    tokens = ring * rows
    for half in range(CORES):
        total = sums[half * tokens : (half + 1) * tokens]
        total = total + sums[(CORES + half) * tokens : (CORES + half + 1) * tokens]
        out_ref[:, :, half * part : (half + 1) * part] = total.reshape(ring, rows, part).astype(BF)


def spread_kernel(parts_ref, out_ref):
    peers, _, part = parts_ref.shape
    for peer in range(peers):
        out_ref[:, peer * part : (peer + 1) * part] = parts_ref[peer]


def stack_pairs(flat_ref, stacked_ref):
    rows = flat_ref.shape[0]
    total, span = stacked_ref.shape
    for p in range(0, total // rows, 2):
        both = [flat_ref[:, q * span : (q + 1) * span].astype(F32) for q in (p, p + 1)]
        stacked_ref[p * rows : (p + 2) * rows, :] = jnp.concatenate(both, axis=0).astype(BF)


def unstack_pairs(stacked, flat_ref):
    rows = flat_ref.shape[0]
    total, span = stacked.shape
    for p in range(total // rows):
        flat_ref[:, p * span : (p + 1) * span] = stacked[p * rows : (p + 1) * rows].astype(BF)


def pack_kernel(asked_ref, cache_ref, *refs):
    out_refs, stacked_ref = refs[:-1], refs[-1]
    rows = len(out_refs)
    pairs, span = out_refs[0].shape
    stack_pairs(cache_ref, stacked_ref)
    pair, column = iota((pairs, pairs * rows), 0), iota((pairs, pairs * rows), 1)
    same_pair = column // rows == pair
    select = [
        jnp.where(same_pair & (column % rows == asked_ref[r]), 1.0, 0.0) for r in range(rows)
    ]
    select = jnp.concatenate(select, axis=0).astype(BF)
    packed = dot(select, stacked_ref[...])
    for r, out_ref in enumerate(out_refs):
        out_ref[...] = packed[r * pairs : (r + 1) * pairs].astype(BF)


def attend_kernel(
    source_ref, length_ref, new_ref, queries_ref, *refs
):
    cache_ref, mixed_ref, token_ref, arrived_ref, stacked_ref, keys_ref, out_ref = refs[-7:]
    token_ref[...] = jnp.zeros(token_ref.shape, F32)
    rows, pairs, span = arrived_ref.shape
    for d, moved_ref in enumerate(refs[:-7]):
        arrived_ref[d] = moved_ref[...].astype(F32)
    width = span // 2
    reach = -(-width // 128) * 128
    total = rows * pairs
    one, two = iota((total, total), 0), iota((total, total), 1)
    to_rows = (one // pairs == two % rows) & (one % pairs == two // rows)
    to_rows = jnp.where(to_rows, 1.0, 0.0).astype(BF)
    to_pairs = (one // rows == two % pairs) & (one % rows == two // pairs)
    to_pairs = jnp.where(to_pairs, 1.0, 0.0).astype(BF)
    stack_pairs(queries_ref, stacked_ref)
    queries = dot(to_rows, stacked_ref[...])
    turned = pltpu.roll(queries, width, 1)
    inside = iota((2 * pairs, reach), 1) < width
    pair, lane = iota((pairs, span), 0), iota((pairs, span), 1)
    column = iota((2 * pairs, 2 * pairs), 1)
    position = 2 * (column % pairs) + column // pairs
    for j in range(rows):
        length = length_ref[j]
        keys = arrived_ref[source_ref[j]]
        placed = (pair == length // 2) & ((lane >= width) == (length % 2 == 1))
        keys = jnp.where(placed, new_ref[j : j + 1, :], keys)
        keys_ref[j * pairs : (j + 1) * pairs, :] = keys.astype(BF)
        both = jnp.concatenate([keys, pltpu.roll(keys, width, 1)], axis=0)[:, 0:reach].astype(BF)
        own = slice(j * pairs, (j + 1) * pairs)
        heads = jnp.concatenate([queries[own, 0:reach], turned[own, 0:reach]], axis=0)
        heads = jnp.where(inside, heads, 0.0).astype(BF)
        scores = dot(heads, both, ((1,), (1,))) * score_scale
        scores = jnp.where(position <= length, scores, -jnp.inf)
        raised = jnp.exp(scores - jnp.max(scores, axis=1, keepdims=True))
        weights = (raised / jnp.sum(raised, axis=1, keepdims=True)).astype(BF)
        mixed = dot(weights, both[:, 0:LAT])
        mixed = jnp.concatenate([mixed[0:pairs], mixed[pairs:]], axis=1)
        out_ref[j * pairs : (j + 1) * pairs, :] = mixed.astype(BF)
    unstack_pairs(dot(to_pairs, keys_ref[...]), cache_ref)
    unstack_pairs(dot(to_pairs, out_ref[...]), mixed_ref)


def call(kernel, out_shape, in_specs, name, scratch=(), after=(), limit=32):
    count = len(in_specs)

    def body(*refs):
        kernel(*refs[:count], *refs[count + len(after) :])

    return lambda *args: pl.pallas_call(
        body,
        out_shape=out_shape,
        in_specs=in_specs + [VMEM] * len(after),
        out_specs=jax.tree.map(lambda _: VMEM, out_shape),
        scratch_shapes=list(scratch),
        compiler_params=pltpu.CompilerParams(vmem_limit_bytes=limit * MIB),
        name=name,
    )(*args, *after)


TOKEN = jax.ShapeDtypeStruct((8, 128), F32)


def on_device(
    latent_cache,
    old_slot,
    lengths,
    new_latent,
    queries,
    hidden,
    expert_ids,
    expert_gates,
    gate_weight,
    up_weight,
    down_weight,
):
    rows, features = hidden.shape
    top = expert_ids.shape[1]
    peers = lax.axis_size("req")
    experts = lax.axis_size("exp")
    ring = peers // CORES
    part = features // ring
    inner = gate_weight.shape[2]
    me = lax.axis_index("req").astype(jnp.int32)
    place = jnp.stack([me // CORES, me % CORES])
    swap = [(k, k ^ 1) for k in range(peers)]
    same_core = [[k for k in range(peers) if k % CORES == c] for c in range(CORES)]

    def along(d):
        return [(k, (k + CORES * d) % peers) for k in range(peers)]

    def exchange_y(x):
        return lax.all_to_all(
            x, "req", split_axis=0, concat_axis=0, tiled=True, axis_index_groups=same_core
        )

    column_span = experts * rows
    message = call(
        functools.partial(announce_kernel, column_span),
        shape_of((ring, rows, part + NOTE)),
        [ANY] * 4,
        "announce",
        [
            pltpu.SMEM(old_slot.shape, jnp.int32),
            pltpu.VMEM(hidden.shape, BF),
            pltpu.VMEM(expert_ids.shape, jnp.int32),
            pltpu.VMEM(expert_gates.shape, F32),
            pltpu.SemaphoreType.DMA((4,)),
        ],
        limit=56,
    )(old_slot, hidden, expert_ids, expert_gates)
    arrived = exchange_y(message)

    own_weights = [w[0] for w in (gate_weight, up_weight, down_weight)]
    sibling_weights = [lax.ppermute(w, "req", swap) for w in own_weights]

    width = new_latent.shape[1]
    span = 2 * width
    pairs = latent_cache.shape[1] // span
    asked = arrived[:, 0, part + 4 * top : part + 4 * top + CORES].astype(jnp.int32)
    asked = asked.T
    core = place[1]
    other = lax.ppermute(lax.dynamic_index_in_dim(asked, 1 - core, 0, False), "req", swap)
    asked = lax.dynamic_index_in_dim(asked, core, 0, False)
    asked = jnp.where(core == 0, jnp.stack([asked, other], 1), jnp.stack([other, asked], 1))
    asked = jnp.roll(asked.reshape(-1), -me)
    packed = call(
        pack_kernel,
        [shape_of((pairs, span))] * peers,
        [SMEM, VMEM],
        "pack",
        [pltpu.VMEM((rows * pairs, span), BF)],
    )(asked, latent_cache)
    moved = [packed[0]] + [
        lax.ppermute(packed[d], "req", [(k, (k + d) % peers) for k in range(peers)])
        for d in range(1, peers)
    ]
    new_pair = jnp.concatenate([new_latent, new_latent], axis=1).astype(F32)
    source = lax.rem(me - old_slot // column_span + peers, peers)
    cache_out, attention, done = call(
        attend_kernel,
        [shape_of(latent_cache.shape), shape_of((rows, pairs * 2 * LAT)), TOKEN],
        [SMEM, SMEM, VMEM, VMEM] + [VMEM] * peers,
        "attend",
        [
            pltpu.VMEM((rows, pairs, span), F32),
            pltpu.VMEM((rows * pairs, span), BF),
            pltpu.VMEM((rows * pairs, span), BF),
            pltpu.VMEM((rows * pairs, 2 * LAT), BF),
        ],
    )(source, lengths, new_pair, queries, *moved)


    slots = CAP * ring
    outgoing = call(
        functools.partial(route_kernel, top),
        shape_of((experts, CORES * slots, part // CORES)),
        [VMEM],
        "route",
        limit=ROUTE,
    )(arrived)
    received = lax.all_to_all(outgoing, "exp", split_axis=0, concat_axis=0, tiled=True)
    weights = call(
        functools.partial(weigh_kernel, top, experts),
        shape_of((experts * CORES * slots, 2 * CORES * ring * rows)),
        [VMEM],
        "weigh",
    )(arrived)

    size = experts // ring * slots
    tile = inner // TILES
    width_own = part // CORES
    column = pl.BlockSpec((width_own, tile), lambda i: (0, i))
    sums_spec = [pl.BlockSpec((size, tile), lambda i: (0, i))] * ring
    sums_shape = [shape_of((size, inner))] * ring
    rows_spec = [pl.BlockSpec((ring * size, width_own), lambda i: (0, 0))] * 2
    params = pltpu.CompilerParams(vmem_limit_bytes=PART * MIB)
    mine, theirs, *gates = pl.pallas_call(
        lambda *refs: gate_kernel(*refs[:4], *refs[6:]),
        grid=(TILES,),
        out_shape=[shape_of((ring * size, width_own))] * 2 + sums_shape,
        in_specs=[SMEM, pl.BlockSpec(received.shape, lambda i: (0, 0, 0))] + [column] * 2 + [ANY] * 2,
        out_specs=rows_spec + sums_spec,
        compiler_params=params,
        name="gate",
    )(place, received, own_weights[0], sibling_weights[0], done, weights)
    ups = pl.pallas_call(
        up_kernel,
        grid=(TILES,),
        out_shape=sums_shape,
        in_specs=rows_spec + [column] * 2,
        out_specs=sums_spec,
        compiler_params=params,
        name="up",
    )(mine, theirs, own_weights[1], sibling_weights[1])
    sent = [gates[0], ups[0]]
    for d in sorted(range(1, ring), key=lambda d: -min(d, ring - d)):
        sent += [lax.ppermute(x[d], "req", along(d)) for x in (gates, ups)]
    units = call(units_kernel, shape_of((ring, size, inner)), [VMEM] * (2 * ring), "units")(*sent)
    result = call(
        down_kernel,
        shape_of(received.shape),
        [SMEM] + [VMEM] * 3,
        "down",
        limit=DOWN,
    )(place, exchange_y(units), own_weights[2], sibling_weights[2])
    returned = lax.all_to_all(result, "exp", split_axis=0, concat_axis=0, tiled=True)
    combined = call(combine_kernel, shape_of((ring, rows, part)), [VMEM] * 2, "combine")(
        weights, returned
    )
    moe_out = call(spread_kernel, shape_of((rows, features)), [VMEM], "spread")(
        exchange_y(combined)
    )

    return (cache_out, attention, moe_out)


def solution(mesh):
    in_specs = (
        P(("req", "exp"), None),
        P(("req", "exp")),
        P(("req", "exp")),
        P(("req", "exp"), None),
        P(("req", "exp"), None),
        P(("req", "exp"), None),
        P(("req", "exp"), None),
        P(("req", "exp"), None),
        P("exp", "req", None),
        P("exp", "req", None),
        P("exp", None, "req"),
    )
    out_specs = (P(("req", "exp"), None), P(("req", "exp"), None), P(("req", "exp"), None))
    return jax.shard_map(
        on_device, mesh=mesh, in_specs=in_specs, out_specs=out_specs, check_vma=False
    )
```
